32 devices in a mesh: dp: 32 (over z, y, x, core).
Axes of the slice: x: 2, y: 2, z: 4, core: 2. Of those that a mesh axis runs over, the one named last changes fastest.
Arguments:
- images: bfloat16 [8192, 1152], P('dp'), may hold values from -6 to 6
- texts: bfloat16 [8192, 1152], P('dp'), may hold values from -6 to 6
- plan: int32 [2, 32], replicated, may hold values from 0 to 31, as said below
Outputs:
- row_loss: float32 [8192], P('dp')
- image_grad: bfloat16 [8192, 1152], P('dp')
- text_grad: bfloat16 [8192, 1152], P('dp')
The draws below stay inside these ranges and needn't reach their ends.
Inputs may be any that keep to these rules, and one draw needn't show every extreme that they name: `plan`: in round r every block's partner is its index XOR a mask m_r common to all blocks, whose highest set bit is bit log2(32) - 1 - r; so partners pair up mutually, differ from the block itself, and differ between rounds.
All inputs are finite; a program needn't handle non-finite values.
Results may differ from the reference program's by a relative error of at most 0.0052.
Values may be sent and summed in bfloat16 or wider, within the bound.
A program may use at most 64 MiB of HBM per device.

```python
import jax
import jax.numpy as jnp
from jax import lax

D = 1152
ROWS = 256
ROUNDS = 2
PLAYERS = 32
BATCH = 8192


def draw_plan(key, part):
    key = jax.random.fold_in(key, 7)
    nbits = PLAYERS.bit_length() - 1
    masks = []
    for rr in range(ROUNDS):
        level = nbits - 1 - rr
        sub = jax.random.fold_in(key, 100 + rr)
        masks.append(jax.random.randint(sub, (), 2 ** level, 2 ** (level + 1), dtype=jnp.int32))
    stacked = jnp.stack(masks).astype(jnp.int32)
    players = jnp.arange(PLAYERS, dtype=jnp.int32)
    return jnp.bitwise_xor(players[None, :], stacked[:, None]).astype(jnp.int32)


def levels(own_key, extent, shards, least, largest):
    factor_of = 1.0
    for position, shards_of in shards:
        steps = jax.random.uniform(jax.random.fold_in(jax.random.fold_in(own_key, 6), position), (shards_of,), jnp.float32, least / len(shards), largest / len(shards))
        factor_of = factor_of * jnp.repeat(jnp.exp(steps), extent[position] // shards_of).reshape((-1,) + (1,) * (len(extent) - 1 - position))
    return factor_of


def normal_values(rng, extent, scale, limit, cuts=(), kind=jnp.bfloat16):
    loudness = levels(rng, extent, cuts, -0.22, 0.18) if cuts else 1.0
    array = jax.random.normal(rng, extent, jnp.float32) * scale * loudness
    return jnp.minimum(jnp.maximum(array, -limit), limit).astype(kind)


def setup_inputs(seed: int = 0) -> dict:
    key_of = jax.random.split(jax.random.key(seed), 4)
    return {
        "images": normal_values(key_of[0], (BATCH, D), 1.0, 6.0, ((0, 32),)),
        "texts": normal_values(key_of[1], (BATCH, D), 1.0, 6.0, ((0, 32),)),
        "plan": draw_plan(jax.random.fold_in(key_of[3], 71), 0),
    }


TEMPER = 2.0
OFFSET = -1.0


def tile_terms(img, txt, labels, scale):
    z = jnp.dot(img, txt.T, preferred_element_type=jnp.float32) * scale + OFFSET
    loss = jnp.sum(jnp.logaddexp(jnp.float32(0.0), -labels * z), axis=1)
    g = (-labels * jax.nn.sigmoid(-labels * z)).astype(jnp.bfloat16)
    img_part = jnp.dot(g, txt, preferred_element_type=jnp.float32) * scale
    txt_part = lax.dot_general(g, img, (((0,), (0,)), ((), ())), preferred_element_type=jnp.float32) * scale
    return loss, img_part, txt_part


def reference(images, texts, plan):
    width = images.shape[1]
    scale = TEMPER / (width ** 0.5)
    img_blocks = images.reshape(PLAYERS, ROWS, width)
    txt_blocks = texts.reshape(PLAYERS, ROWS, width)
    eye = jnp.eye(ROWS, dtype=jnp.float32)
    diag_labels = 2.0 * eye - 1.0
    neg_labels = jnp.zeros((ROWS, ROWS), jnp.float32) - 1.0

    def per_block(q):
        own_img = img_blocks[q]
        loss, igrad, tgrad = tile_terms(own_img, txt_blocks[q], diag_labels, scale)
        sent = []
        for rr in range(ROUNDS):
            partner = plan[rr, q]
            l2, ig2, tp = tile_terms(own_img, txt_blocks[partner], neg_labels, scale)
            loss = loss + l2
            igrad = igrad + ig2
            sent.append(tp.astype(jnp.bfloat16))
        return loss, igrad.astype(jnp.bfloat16), tgrad, tuple(sent)

    loss, igrad, tgrad, sent = lax.map(per_block, jnp.arange(PLAYERS, dtype=jnp.int32))
    for rr in range(ROUNDS):
        tgrad = tgrad + sent[rr][plan[rr]].astype(jnp.float32)
    row_loss = (loss / ((ROUNDS + 1) * ROWS)).reshape(PLAYERS * ROWS)
    return row_loss, igrad.reshape(PLAYERS * ROWS, width), tgrad.astype(jnp.bfloat16).reshape(PLAYERS * ROWS, width)
```

```python
import jax
import jax.numpy as jnp
from jax import lax
from jax.sharding import PartitionSpec as P

ROUNDS = 2
TEMPER = 2.0
OFFSET = -1.0
ONE_HOP = 4


def tile_coeffs(img, txt, labels, scale):
    z = jnp.dot(img, txt.T, preferred_element_type=jnp.float32) * scale + OFFSET
    loss = jnp.sum(jnp.logaddexp(jnp.float32(0.0), -labels * z), axis=1)
    g = (-labels * jax.nn.sigmoid(-labels * z)).astype(jnp.bfloat16)
    return (loss, g)


def coeffs(img, txt, labels, scale):
    z = jnp.dot(img, txt.T, preferred_element_type=jnp.float32) * scale + OFFSET
    return (-labels * jax.nn.sigmoid(-labels * z)).astype(jnp.bfloat16)


def image_side(g, txt, scale):
    return jnp.dot(g, txt, preferred_element_type=jnp.float32) * scale


def text_side(g, img, scale):
    return (
        lax.dot_general(g, img, (((0,), (0,)), ((), ())), preferred_element_type=jnp.float32)
        * scale
    )


def send_pairs(masks, *blocks):
    devices = range(lax.axis_size("dp"))
    return tuple(
        lax.ppermute(block, "dp", [(source, source ^ mask) for source in devices])
        if mask
        else block
        for block, mask in zip(blocks, masks)
    )


def exchange(images, texts, flips):
    nbits = lax.axis_size("dp").bit_length() - 1
    free = [nbits - 1 - rr for rr in range(ROUNDS)]
    digit_bits = ONE_HOP if max(free) <= ONE_HOP else 3
    held = (images, texts) * ROUNDS
    low = 0
    while low < max(free):
        widths = [max(0, min(digit_bits, bits - low)) for bits in free]
        last = low + digit_bits >= max(free)
        index, count = jnp.int32(0), 1
        for rr, width in enumerate(widths):
            digit = jnp.bitwise_and(jnp.right_shift(flips[rr], low), 2**width - 1)
            index, count = index + digit * count, count * 2**width
        branches = []
        for branch in range(count):
            masks = []
            for bits, width in zip(free, widths):
                mask = (branch % 2**width) << low
                branch //= 2**width
                masks += [mask + (2**bits if last else 0)] * 2
            branches.append(lambda *blocks, masks=tuple(masks): send_pairs(masks, *blocks))
        held = lax.switch(index, branches, *held)
        low += digit_bits
    return [(held[2 * rr], held[2 * rr + 1]) for rr in range(ROUNDS)]


def shards(images, texts, plan):
    rows_here, width = images.shape
    scale = TEMPER / width**0.5
    position = lax.axis_index("dp")
    flips = [jnp.bitwise_xor(plan[rr, position], position) for rr in range(ROUNDS)]
    eye = jnp.eye(rows_here, dtype=jnp.float32)
    diag_labels = 2.0 * eye - 1.0
    neg_labels = jnp.zeros((rows_here, rows_here), jnp.float32) - 1.0
    theirs = exchange(images, texts, flips)
    loss, g_diag = tile_coeffs(images, texts, diag_labels, scale)
    igrad = image_side(g_diag, texts, scale)
    tgrad = text_side(g_diag, images, scale)
    for other_img, other_txt in theirs:
        l2, g_mine = tile_coeffs(images, other_txt, neg_labels, scale)
        loss = loss + l2
        igrad = igrad + image_side(g_mine, other_txt, scale)
        g_theirs = coeffs(other_img, texts, neg_labels, scale)
        partial = text_side(g_theirs, other_img, scale).astype(jnp.bfloat16)
        tgrad = tgrad + partial.astype(jnp.float32)
    row_loss = loss / ((ROUNDS + 1) * rows_here)
    return (row_loss, igrad.astype(jnp.bfloat16), tgrad.astype(jnp.bfloat16))


def solution(mesh):
    placed = (P("dp", None), P("dp", None), P())
    return jax.shard_map(
        shards,
        mesh=mesh,
        in_specs=placed,
        out_specs=(P("dp"), P("dp", None), P("dp", None)),
        check_vma=False,
    )
```

```python
import functools

import jax
import jax.numpy as jnp
from jax import lax
from jax.experimental import pallas as pl
from jax.experimental.pallas import tpu as pltpu
from jax.sharding import PartitionSpec as P

MESH = pl.DeviceIdType.MESH
ROUNDS = 2
TEMPER = 2.0
OFFSET = -1.0
KERNEL_DEVICES = 32
CORE, FIRST, SECOND, NEAR, FAR = 1, 2, 4, 8, 16
PARTS = 4
CHUNKS = 2 * PARTS
HOP_BITS = 2


def flip(index, bit):
    return index + bit - 2 * bit * ((index // bit) % 2)


def pick(own, other, taken):
    mixed = own.astype(jnp.float32) * (1.0 - taken) + other.astype(jnp.float32) * taken
    return mixed.astype(jnp.bfloat16)


def loss_and_slope(t):
    e = jnp.exp(-jnp.abs(t))
    r = 1.0 / (1.0 + e)
    return jnp.maximum(t, 0.0) + jnp.log1p(e), jnp.where(t >= 0.0, r, e * r)


def logits(img, txt, scale):
    dims = (((1,), (1,)), ((), ()))
    return lax.dot_general(img, txt, dims, preferred_element_type=jnp.float32) * scale + OFFSET


def over_rows(g, img):
    return lax.dot_general(g, img, (((0,), (0,)), ((), ())), preferred_element_type=jnp.float32)


def kernel(
    far_bits, scale, taken, img, txt, loss_out, igrad_out, tgrad_out,
    a_recv, b_send, b_recv, c_send, c_recv, d_recv, other, losses, igrad, tgrad,
    a_sems, b_sems, c_sems, d_sems,
):
    me = lax.axis_index("dp")
    core, first, second, near = (flip(me, bit) for bit in (CORE, FIRST, SECOND, NEAR))
    far = me
    for bit in far_bits:
        far = flip(far, bit)
    rows = img.shape[0]
    part = rows // PARTS

    barrier = pltpu.get_barrier_semaphore()
    for device in (core, first, second, near, far):
        pl.semaphore_signal(barrier, inc=1, device_id=(device,), device_id_type=MESH)
    pl.semaphore_wait(barrier, 5)

    def copy(src, dst, sems, place, device):
        return pltpu.make_async_remote_copy(
            src_ref=src, dst_ref=dst, send_sem=sems.at[(0, *place)], recv_sem=sems.at[(1, *place)],
            device_id=(device,), device_id_type=MESH,
        )

    def own(j):
        return (txt if j < PARTS else img).at[pl.ds((j % PARTS) * part, part)]

    order = [(first, second) if j % 2 == 0 else (second, first) for j in range(CHUNKS)]
    bits = [(1, 2) if j % 2 == 0 else (2, 1) for j in range(CHUNKS)]
    a = [copy(own(j), a_recv.at[j], a_sems, (j,), order[j][0]) for j in range(CHUNKS)]
    b = [copy(b_send.at[j], b_recv.at[j], b_sems, (j,), order[j][1]) for j in range(CHUNKS)]
    c = [
        [copy(c_send.at[j, rr], c_recv.at[j, rr], c_sems, (j, rr), (far, near)[rr]) for rr in range(ROUNDS)]
        for j in range(CHUNKS)
    ]
    d = [copy(c_recv.at[j], d_recv.at[j], d_sems, (j,), core) for j in range(CHUNKS)]

    def diagonal():
        z = logits(img[...], txt[...], scale)
        shape = (rows, rows)
        same = lax.broadcasted_iota(jnp.int32, shape, 0) == lax.broadcasted_iota(jnp.int32, shape, 1)
        loss, slope = loss_and_slope(jnp.where(same, -z, z))
        losses[...] = loss
        g = jnp.where(same, -slope, slope).astype(jnp.bfloat16)
        igrad[...] = jnp.dot(g, txt[...], preferred_element_type=jnp.float32)
        tgrad[...] = over_rows(g, img[...])

    a[0].start()
    a[1].start()
    for j in range(CHUNKS + 1):
        if j < CHUNKS:
            a[j].wait_recv()
            for rr in range(ROUNDS):
                b_send[j, rr] = pick(own(j)[...], a_recv[j], taken[rr, bits[j][0]])
            b[j].start()
            if j + 2 < CHUNKS:
                a[j + 2].start()
        if j >= 1:
            b[j - 1].wait_recv()
            for rr in range(ROUNDS):
                c_send[j - 1, rr] = pick(b_send[j - 1, rr], b_recv[j - 1, rr], taken[rr, bits[j - 1][1]])
                c[j - 1][rr].start()
        if j == 3:
            diagonal()

    def finish(j):
        d[j].wait_recv()
        for rr in range(ROUNDS):
            arrived = pick(c_recv[j, rr], d_recv[j, rr], taken[rr, 0])
            if j < PARTS:
                other[rr, pl.ds(j * part, part)] = arrived
            else:
                _, slope = loss_and_slope(logits(arrived, txt[...], scale))
                tgrad[...] += over_rows(slope.astype(jnp.bfloat16), arrived)
        if j == PARTS - 1:
            for rr in range(ROUNDS):
                loss, slope = loss_and_slope(logits(img[...], other[rr], scale))
                losses[...] += loss
                igrad[...] += jnp.dot(slope.astype(jnp.bfloat16), other[rr], preferred_element_type=jnp.float32)
            igrad_out[...] = (igrad[...] * scale).astype(jnp.bfloat16)
            total = jnp.sum(losses[...].T, axis=0, keepdims=True)
            loss_out[...] = total / ((ROUNDS + 1) * rows)

    for j in range(CHUNKS + 1):
        if j < CHUNKS:
            for rr in range(ROUNDS):
                c[j][rr].wait_recv()
            d[j].start()
        if j >= 1:
            finish(j - 1)
    tgrad_out[...] = (tgrad[...] * scale).astype(jnp.bfloat16)
    for j in range(CHUNKS):
        for sent in (a[j], b[j], c[j][0], c[j][1], d[j]):
            sent.wait_send()


def whole_step(variant, scale, taken, images, texts):
    rows, width = images.shape
    part = rows // PARTS
    vmem = pl.BlockSpec(memory_space=pltpu.VMEM)
    both = pltpu.VMEM((CHUNKS, ROUNDS, part, width), jnp.bfloat16)
    total = pltpu.VMEM((rows, width), jnp.float32)
    far_bits = (FAR, NEAR) if variant else (FAR,)
    return pl.pallas_call(
        functools.partial(kernel, far_bits, scale),
        out_shape=(
            jax.ShapeDtypeStruct((1, rows), jnp.float32),
            jax.ShapeDtypeStruct((rows, width), jnp.bfloat16),
            jax.ShapeDtypeStruct((rows, width), jnp.bfloat16),
        ),
        in_specs=[pl.BlockSpec(memory_space=pltpu.SMEM), vmem, vmem],
        out_specs=(vmem, vmem, vmem),
        scratch_shapes=[
            pltpu.VMEM((CHUNKS, part, width), jnp.bfloat16), both, both, both, both, both,
            pltpu.VMEM((ROUNDS, rows, width), jnp.bfloat16), pltpu.VMEM((rows, rows), jnp.float32), total, total,
            pltpu.SemaphoreType.DMA((2, CHUNKS)), pltpu.SemaphoreType.DMA((2, CHUNKS)),
            pltpu.SemaphoreType.DMA((2, CHUNKS, ROUNDS)), pltpu.SemaphoreType.DMA((2, CHUNKS)),
        ],
        compiler_params=pltpu.CompilerParams(
            collective_id=variant, has_side_effects=True, vmem_limit_bytes=48 * 2**20
        ),
        cost_estimate=pl.CostEstimate(flops=22 * rows * rows * width, bytes_accessed=8 * rows * width, transcendentals=0),
    )(taken, images, texts)


def kernel_shards(images, texts, plan):
    rows, width = images.shape
    scale = TEMPER / width**0.5
    flipped = jnp.bitwise_xor(plan[:, 0], 0)
    shifts = jnp.arange(3, dtype=jnp.int32)
    taken = jnp.bitwise_and(jnp.right_shift(flipped[:, None], shifts[None, :]), 1).astype(jnp.float32)
    crosses = jnp.bitwise_and(flipped[0], NEAR) != 0
    loss, igrad, tgrad = lax.cond(
        crosses, functools.partial(whole_step, 1, scale), functools.partial(whole_step, 0, scale), taken, images, texts
    )
    return loss.reshape(rows), igrad, tgrad


def tile_coeffs(img, txt, labels, scale):
    z = jnp.dot(img, txt.T, preferred_element_type=jnp.float32) * scale + OFFSET
    loss = jnp.sum(jnp.logaddexp(jnp.float32(0.0), -labels * z), axis=1)
    g = (-labels * jax.nn.sigmoid(-labels * z)).astype(jnp.bfloat16)
    return (loss, g)


def coeffs(img, txt, labels, scale):
    z = jnp.dot(img, txt.T, preferred_element_type=jnp.float32) * scale + OFFSET
    return (-labels * jax.nn.sigmoid(-labels * z)).astype(jnp.bfloat16)


def image_side(g, txt, scale):
    return jnp.dot(g, txt, preferred_element_type=jnp.float32) * scale


def text_side(g, img, scale):
    return (
        lax.dot_general(g, img, (((0,), (0,)), ((), ())), preferred_element_type=jnp.float32)
        * scale
    )


def send_pairs(masks, *blocks):
    devices = range(lax.axis_size("dp"))
    return tuple(
        lax.ppermute(block, "dp", [(source, source ^ mask) for source in devices])
        if mask
        else block
        for block, mask in zip(blocks, masks)
    )


def exchange(images, texts, flips):
    nbits = lax.axis_size("dp").bit_length() - 1
    free = [nbits - 1 - rr for rr in range(ROUNDS)]
    digit_bits = HOP_BITS
    held = (images, texts) * ROUNDS
    low = 0
    while low < max(free):
        widths = [max(0, min(digit_bits, bits - low)) for bits in free]
        last = low + digit_bits >= max(free)
        index, count = jnp.int32(0), 1
        for rr, width in enumerate(widths):
            digit = jnp.bitwise_and(jnp.right_shift(flips[rr], low), 2**width - 1)
            index, count = index + digit * count, count * 2**width
        branches = []
        for branch in range(count):
            masks = []
            for bits, width in zip(free, widths):
                mask = (branch % 2**width) << low
                branch //= 2**width
                masks += [mask + (2**bits if last else 0)] * 2
            branches.append(lambda *blocks, masks=tuple(masks): send_pairs(masks, *blocks))
        held = lax.switch(index, branches, *held)
        low += digit_bits
    return [(held[2 * rr], held[2 * rr + 1]) for rr in range(ROUNDS)]


def hop_shards(images, texts, plan):
    rows_here, width = images.shape
    scale = TEMPER / width**0.5
    position = lax.axis_index("dp")
    flips = [jnp.bitwise_xor(plan[rr, position], position) for rr in range(ROUNDS)]
    eye = jnp.eye(rows_here, dtype=jnp.float32)
    diag_labels = 2.0 * eye - 1.0
    neg_labels = jnp.zeros((rows_here, rows_here), jnp.float32) - 1.0
    theirs = exchange(images, texts, flips)
    loss, g_diag = tile_coeffs(images, texts, diag_labels, scale)
    igrad = image_side(g_diag, texts, scale)
    tgrad = text_side(g_diag, images, scale)
    for other_img, other_txt in theirs:
        l2, g_mine = tile_coeffs(images, other_txt, neg_labels, scale)
        loss = loss + l2
        igrad = igrad + image_side(g_mine, other_txt, scale)
        g_theirs = coeffs(other_img, texts, neg_labels, scale)
        partial = text_side(g_theirs, other_img, scale).astype(jnp.bfloat16)
        tgrad = tgrad + partial.astype(jnp.float32)
    row_loss = loss / ((ROUNDS + 1) * rows_here)
    return (row_loss, igrad.astype(jnp.bfloat16), tgrad.astype(jnp.bfloat16))


def solution(mesh):
    placed = (P("dp", None), P("dp", None), P())
    return jax.shard_map(
        kernel_shards if mesh.shape["dp"] == KERNEL_DEVICES else hop_shards,
        mesh=mesh,
        in_specs=placed,
        out_specs=(P("dp"), P("dp", None), P("dp", None)),
        check_vma=False,
    )
```

```python
import functools

import jax
import jax.numpy as jnp
from jax import lax
from jax.experimental import pallas as pl
from jax.experimental.pallas import tpu as pltpu
from jax.sharding import PartitionSpec as P

MESH = pl.DeviceIdType.MESH
ROUNDS = 2
TEMPER = 2.0
OFFSET = -1.0
KERNEL_DEVICES = 32
CORE, FIRST, SECOND, NEAR, FAR = 1, 2, 4, 8, 16
PARTS = 4
CHUNKS = 2 * PARTS
Z_FIRST = 2
HOP_BITS = 2


def flip(index, bit):
    return index + bit - 2 * bit * ((index // bit) % 2)


def pick(own, other, taken):
    mixed = own.astype(jnp.float32) * (1.0 - taken) + other.astype(jnp.float32) * taken
    return mixed.astype(jnp.bfloat16)


def loss_and_slope(t):
    e = jnp.exp(-jnp.abs(t))
    r = 1.0 / (1.0 + e)
    return jnp.maximum(t, 0.0) + jnp.log1p(e), jnp.where(t >= 0.0, r, e * r)


def logits(img, txt, scale):
    dims = (((1,), (1,)), ((), ()))
    return lax.dot_general(img, txt, dims, preferred_element_type=jnp.float32) * scale + OFFSET


def over_rows(g, img):
    return lax.dot_general(g, img, (((0,), (0,)), ((), ())), preferred_element_type=jnp.float32)


def kernel(
    far_bits, scale, plan, img, txt, loss_out, igrad_out, tgrad_out,
    a_recv, b_send, b_recv, c_send, c_recv, d_recv, e_recv, f_send, f_recv, g_send, other, losses, igrad, tgrad,
    a_sems, b_sems, c_sems, d_sems, e_sems, f_sems,
):
    me = lax.axis_index("dp")
    core, first, second, near = (flip(me, bit) for bit in (CORE, FIRST, SECOND, NEAR))
    far = me
    for bit in far_bits:
        far = flip(far, bit)
    rows = img.shape[0]
    part = rows // PARTS
    taken = [
        [jnp.bitwise_and(lax.shift_right_logical(plan[rr, 0], bit), 1).astype(jnp.float32) for bit in range(3)]
        for rr in range(ROUNDS)
    ]

    barrier = pltpu.get_barrier_semaphore()
    for device in (core, first, second, near, far):
        pl.semaphore_signal(barrier, inc=1, device_id=(device,), device_id_type=MESH)
    pl.semaphore_wait(barrier, 5)

    def copy(src, dst, sems, place, device):
        return pltpu.make_async_remote_copy(
            src_ref=src, dst_ref=dst, send_sem=sems.at[(0, *place)], recv_sem=sems.at[(1, *place)],
            device_id=(device,), device_id_type=MESH,
        )

    def own(j):
        return (txt if j < PARTS else img).at[pl.ds((j % PARTS) * part, part)]

    plane_first, z_first = range(Z_FIRST, CHUNKS), range(Z_FIRST)
    order = [(first, second) if j % 2 == 0 else (second, first) for j in range(CHUNKS)]
    bits = [(1, 2) if j % 2 == 0 else (2, 1) for j in range(CHUNKS)]
    a = {j: copy(own(j), a_recv.at[j], a_sems, (j,), order[j][0]) for j in plane_first}
    b = {j: copy(b_send.at[j], b_recv.at[j], b_sems, (j,), order[j][1]) for j in plane_first}
    c = [
        [
            copy(own(j) if j < Z_FIRST else c_send.at[j, rr], c_recv.at[j, rr], c_sems, (j, rr), (far, near)[rr])
            for rr in range(ROUNDS)
        ]
        for j in range(CHUNKS)
    ]
    e = {j: copy(c_recv.at[j], e_recv.at[j], e_sems, (j,), order[j][0]) for j in z_first}
    f = {j: copy(f_send.at[j], f_recv.at[j], f_sems, (j,), order[j][1]) for j in z_first}
    landed = [g_send.at[j] if j < Z_FIRST else c_recv.at[j] for j in range(CHUNKS)]
    d = [copy(landed[j], d_recv.at[j], d_sems, (j,), core) for j in range(CHUNKS)]

    def diagonal():
        z = logits(img[...], txt[...], scale)
        shape = (rows, rows)
        same = lax.broadcasted_iota(jnp.int32, shape, 0) == lax.broadcasted_iota(jnp.int32, shape, 1)
        loss, slope = loss_and_slope(jnp.where(same, -z, z))
        losses[...] = loss
        g = jnp.where(same, -slope, slope).astype(jnp.bfloat16)
        igrad[...] = jnp.dot(g, txt[...], preferred_element_type=jnp.float32)
        tgrad[...] = over_rows(g, img[...])

    def along_z(j):
        for rr in range(ROUNDS):
            c[j][rr].start()

    def after_z(j):
        for rr in range(ROUNDS):
            c[j][rr].wait_recv()

    for j in z_first:
        along_z(j)
    for j in plane_first[:2]:
        a[j].start()
    diagonal()
    for j in range(Z_FIRST, CHUNKS + 1):
        if j < CHUNKS:
            a[j].wait_recv()
            for rr in range(ROUNDS):
                b_send[j, rr] = pick(own(j)[...], a_recv[j], taken[rr][bits[j][0]])
            b[j].start()
            if j + 2 < CHUNKS:
                a[j + 2].start()
        if j > Z_FIRST:
            b[j - 1].wait_recv()
            for rr in range(ROUNDS):
                c_send[j - 1, rr] = pick(b_send[j - 1, rr], b_recv[j - 1, rr], taken[rr][bits[j - 1][1]])
            along_z(j - 1)
        if j == CHUNKS - 3:
            for k in z_first:
                after_z(k)
                e[k].start()
    for j in z_first:
        e[j].wait_recv()
        for rr in range(ROUNDS):
            f_send[j, rr] = pick(c_recv[j, rr], e_recv[j, rr], taken[rr][bits[j][0]])
        f[j].start()
    for j in range(Z_FIRST, PARTS):
        after_z(j)
        d[j].start()
    for j in z_first:
        f[j].wait_recv()
        for rr in range(ROUNDS):
            g_send[j, rr] = pick(f_send[j, rr], f_recv[j, rr], taken[rr][bits[j][1]])
        d[j].start()

    def arrive(j, rr):
        return pick(landed[j][rr], d_recv[j, rr], taken[rr][0])

    for j in (*range(Z_FIRST, PARTS), *z_first):
        d[j].wait_recv()
        for rr in range(ROUNDS):
            other[rr, pl.ds(j * part, part)] = arrive(j, rr)
    after_z(PARTS)
    d[PARTS].start()
    for rr in range(ROUNDS):
        loss, slope = loss_and_slope(logits(img[...], other[rr], scale))
        losses[...] += loss
        igrad[...] += jnp.dot(slope.astype(jnp.bfloat16), other[rr], preferred_element_type=jnp.float32)
    igrad_out[...] = (igrad[...] * scale).astype(jnp.bfloat16)
    loss_out[...] = jnp.sum(losses[...].T, axis=0, keepdims=True) / ((ROUNDS + 1) * rows)
    for j in range(PARTS, CHUNKS):
        if j + 1 < CHUNKS:
            after_z(j + 1)
            d[j + 1].start()
        d[j].wait_recv()
        for rr in range(ROUNDS):
            arrived = arrive(j, rr)
            _, slope = loss_and_slope(logits(arrived, txt[...], scale))
            tgrad[...] += over_rows(slope.astype(jnp.bfloat16), arrived)
    tgrad_out[...] = (tgrad[...] * scale).astype(jnp.bfloat16)
    for j in range(CHUNKS):
        for sent in (*((e[j], f[j]) if j < Z_FIRST else (a[j], b[j])), *c[j], d[j]):
            sent.wait_send()


def whole_step(variant, scale, plan, images, texts):
    rows, width = images.shape
    part = rows // PARTS
    vmem = pl.BlockSpec(memory_space=pltpu.VMEM)
    both = pltpu.VMEM((CHUNKS, ROUNDS, part, width), jnp.bfloat16)
    early = pltpu.VMEM((Z_FIRST, ROUNDS, part, width), jnp.bfloat16)
    total = pltpu.VMEM((rows, width), jnp.float32)
    far_bits = (FAR, NEAR) if variant else (FAR,)
    return pl.pallas_call(
        functools.partial(kernel, far_bits, scale),
        out_shape=(
            jax.ShapeDtypeStruct((1, rows), jnp.float32),
            jax.ShapeDtypeStruct((rows, width), jnp.bfloat16),
            jax.ShapeDtypeStruct((rows, width), jnp.bfloat16),
        ),
        in_specs=[pl.BlockSpec(memory_space=pltpu.SMEM), vmem, vmem],
        out_specs=(vmem, vmem, vmem),
        scratch_shapes=[
            pltpu.VMEM((CHUNKS, part, width), jnp.bfloat16), both, both, both, both, both, early, early, early, early,
            pltpu.VMEM((ROUNDS, rows, width), jnp.bfloat16), pltpu.VMEM((rows, rows), jnp.float32), total, total,
            pltpu.SemaphoreType.DMA((2, CHUNKS)), pltpu.SemaphoreType.DMA((2, CHUNKS)),
            pltpu.SemaphoreType.DMA((2, CHUNKS, ROUNDS)), pltpu.SemaphoreType.DMA((2, CHUNKS)),
            pltpu.SemaphoreType.DMA((2, Z_FIRST)), pltpu.SemaphoreType.DMA((2, Z_FIRST)),
        ],
        compiler_params=pltpu.CompilerParams(
            collective_id=variant, has_side_effects=True, vmem_limit_bytes=48 * 2**20
        ),
        cost_estimate=pl.CostEstimate(flops=22 * rows * rows * width, bytes_accessed=8 * rows * width, transcendentals=0),
    )(plan, images, texts)


def kernel_shards(images, texts, plan):
    rows, width = images.shape
    scale = TEMPER / width**0.5
    crosses = jnp.bitwise_and(plan[0, 0], NEAR) != 0
    loss, igrad, tgrad = lax.cond(
        crosses, functools.partial(whole_step, 1, scale), functools.partial(whole_step, 0, scale), plan, images, texts
    )
    return loss.reshape(rows), igrad, tgrad


def tile_coeffs(img, txt, labels, scale):
    z = jnp.dot(img, txt.T, preferred_element_type=jnp.float32) * scale + OFFSET
    loss = jnp.sum(jnp.logaddexp(jnp.float32(0.0), -labels * z), axis=1)
    g = (-labels * jax.nn.sigmoid(-labels * z)).astype(jnp.bfloat16)
    return (loss, g)


def coeffs(img, txt, labels, scale):
    z = jnp.dot(img, txt.T, preferred_element_type=jnp.float32) * scale + OFFSET
    return (-labels * jax.nn.sigmoid(-labels * z)).astype(jnp.bfloat16)


def image_side(g, txt, scale):
    return jnp.dot(g, txt, preferred_element_type=jnp.float32) * scale


def text_side(g, img, scale):
    return (
        lax.dot_general(g, img, (((0,), (0,)), ((), ())), preferred_element_type=jnp.float32)
        * scale
    )


def send_pairs(masks, *blocks):
    devices = range(lax.axis_size("dp"))
    return tuple(
        lax.ppermute(block, "dp", [(source, source ^ mask) for source in devices])
        if mask
        else block
        for block, mask in zip(blocks, masks)
    )


def exchange(images, texts, flips):
    nbits = lax.axis_size("dp").bit_length() - 1
    free = [nbits - 1 - rr for rr in range(ROUNDS)]
    digit_bits = HOP_BITS
    held = (images, texts) * ROUNDS
    low = 0
    while low < max(free):
        widths = [max(0, min(digit_bits, bits - low)) for bits in free]
        last = low + digit_bits >= max(free)
        index, count = jnp.int32(0), 1
        for rr, width in enumerate(widths):
            digit = jnp.bitwise_and(jnp.right_shift(flips[rr], low), 2**width - 1)
            index, count = index + digit * count, count * 2**width
        branches = []
        for branch in range(count):
            masks = []
            for bits, width in zip(free, widths):
                mask = (branch % 2**width) << low
                branch //= 2**width
                masks += [mask + (2**bits if last else 0)] * 2
            branches.append(lambda *blocks, masks=tuple(masks): send_pairs(masks, *blocks))
        held = lax.switch(index, branches, *held)
        low += digit_bits
    return [(held[2 * rr], held[2 * rr + 1]) for rr in range(ROUNDS)]


def hop_shards(images, texts, plan):
    rows_here, width = images.shape
    scale = TEMPER / width**0.5
    position = lax.axis_index("dp")
    flips = [jnp.bitwise_xor(plan[rr, position], position) for rr in range(ROUNDS)]
    eye = jnp.eye(rows_here, dtype=jnp.float32)
    diag_labels = 2.0 * eye - 1.0
    neg_labels = jnp.zeros((rows_here, rows_here), jnp.float32) - 1.0
    theirs = exchange(images, texts, flips)
    loss, g_diag = tile_coeffs(images, texts, diag_labels, scale)
    igrad = image_side(g_diag, texts, scale)
    tgrad = text_side(g_diag, images, scale)
    for other_img, other_txt in theirs:
        l2, g_mine = tile_coeffs(images, other_txt, neg_labels, scale)
        loss = loss + l2
        igrad = igrad + image_side(g_mine, other_txt, scale)
        g_theirs = coeffs(other_img, texts, neg_labels, scale)
        partial = text_side(g_theirs, other_img, scale).astype(jnp.bfloat16)
        tgrad = tgrad + partial.astype(jnp.float32)
    row_loss = loss / ((ROUNDS + 1) * rows_here)
    return (row_loss, igrad.astype(jnp.bfloat16), tgrad.astype(jnp.bfloat16))


def solution(mesh):
    placed = (P("dp", None), P("dp", None), P())
    return jax.shard_map(
        kernel_shards if mesh.shape["dp"] == KERNEL_DEVICES else hop_shards,
        mesh=mesh,
        in_specs=placed,
        out_specs=(P("dp"), P("dp", None), P("dp", None)),
        check_vma=False,
    )
```

```python
import functools

import jax
import jax.numpy as jnp
from jax import lax
from jax.experimental import pallas as pl
from jax.experimental.pallas import tpu as pltpu
from jax.sharding import PartitionSpec as P

MESH = pl.DeviceIdType.MESH
ROUNDS = 2
TEMPER = 2.0
OFFSET = -1.0
KERNEL_DEVICES = 32
CORE, FIRST, SECOND, NEAR, FAR = 1, 2, 4, 8, 16
PARTS = 4
CHUNKS = 2 * PARTS
Z_FIRST = 2
HOP_BITS = 2


def flip(index, bit):
    return index + bit - 2 * bit * ((index // bit) % 2)


def pick(own, other, taken):
    mixed = own.astype(jnp.float32) * (1.0 - taken) + other.astype(jnp.float32) * taken
    return mixed.astype(jnp.bfloat16)


def loss_and_slope(t):
    e = jnp.exp(-jnp.abs(t))
    r = 1.0 / (1.0 + e)
    return jnp.maximum(t, 0.0) + jnp.log1p(e), jnp.where(t >= 0.0, r, e * r)


def logits(img, txt, scale):
    dims = (((1,), (1,)), ((), ()))
    return lax.dot_general(img, txt, dims, preferred_element_type=jnp.float32) * scale + OFFSET


def over_rows(g, img):
    return lax.dot_general(g, img, (((0,), (0,)), ((), ())), preferred_element_type=jnp.float32)


def kernel(
    far_bits, scale, plan, img, txt, loss_out, igrad_out, tgrad_out,
    a_recv, b_send, b_recv, c_send, c_recv, d_recv, e_recv, f_send, f_recv, g_send, other, losses, igrad, tgrad,
    a_sems, b_sems, c_sems, d_sems, e_sems, f_sems,
):
    me = lax.axis_index("dp")
    core, first, second, near = (flip(me, bit) for bit in (CORE, FIRST, SECOND, NEAR))
    far = me
    for bit in far_bits:
        far = flip(far, bit)
    rows = img.shape[0]
    part = rows // PARTS
    taken = [
        [jnp.bitwise_and(lax.shift_right_logical(plan[rr, 0], bit), 1).astype(jnp.float32) for bit in range(3)]
        for rr in range(ROUNDS)
    ]

    barrier = pltpu.get_barrier_semaphore()
    for device in (core, first, second, near, far):
        pl.semaphore_signal(barrier, inc=1, device_id=(device,), device_id_type=MESH)
    pl.semaphore_wait(barrier, 5)

    def copy(src, dst, sems, place, device):
        return pltpu.make_async_remote_copy(
            src_ref=src, dst_ref=dst, send_sem=sems.at[(0, *place)], recv_sem=sems.at[(1, *place)],
            device_id=(device,), device_id_type=MESH,
        )

    def own(j):
        return (txt if j < PARTS else img).at[pl.ds((j % PARTS) * part, part)]

    plane_first, z_first = range(Z_FIRST, CHUNKS), range(Z_FIRST)
    order = [(first, second) if j % 2 == 0 else (second, first) for j in range(CHUNKS)]
    bits = [(1, 2) if j % 2 == 0 else (2, 1) for j in range(CHUNKS)]
    a = {j: copy(own(j), a_recv.at[j], a_sems, (j,), order[j][0]) for j in plane_first}
    b = {j: copy(b_send.at[j], b_recv.at[j], b_sems, (j,), order[j][1]) for j in plane_first}
    c = [
        [
            copy(own(j) if j < Z_FIRST else c_send.at[j, rr], c_recv.at[j, rr], c_sems, (j, rr), (far, near)[rr])
            for rr in range(ROUNDS)
        ]
        for j in range(CHUNKS)
    ]
    e = {j: copy(c_recv.at[j], e_recv.at[j], e_sems, (j,), order[j][0]) for j in z_first}
    f = {j: copy(f_send.at[j], f_recv.at[j], f_sems, (j,), order[j][1]) for j in z_first}
    landed = [g_send.at[j] if j < Z_FIRST else c_recv.at[j] for j in range(CHUNKS)]
    d = [copy(landed[j], d_recv.at[j], d_sems, (j,), core) for j in range(CHUNKS)]

    def diagonal():
        z = logits(img[...], txt[...], scale)
        shape = (rows, rows)
        same = lax.broadcasted_iota(jnp.int32, shape, 0) == lax.broadcasted_iota(jnp.int32, shape, 1)
        loss, slope = loss_and_slope(jnp.where(same, -z, z))
        losses[...] = loss
        g = jnp.where(same, -slope, slope).astype(jnp.bfloat16)
        igrad[...] = jnp.dot(g, txt[...], preferred_element_type=jnp.float32)
        tgrad[...] = over_rows(g, img[...])

    def along_z(j):
        for rr in range(ROUNDS):
            c[j][rr].start()

    def after_z(j):
        for rr in range(ROUNDS):
            c[j][rr].wait_recv()

    for j in z_first:
        along_z(j)
    for j in plane_first[:2]:
        a[j].start()
    diagonal()
    for j in range(Z_FIRST, CHUNKS + 1):
        if j < CHUNKS:
            a[j].wait_recv()
            for rr in range(ROUNDS):
                b_send[j, rr] = pick(own(j)[...], a_recv[j], taken[rr][bits[j][0]])
            b[j].start()
            if j + 2 < CHUNKS:
                a[j + 2].start()
        if j > Z_FIRST:
            b[j - 1].wait_recv()
            for rr in range(ROUNDS):
                c_send[j - 1, rr] = pick(b_send[j - 1, rr], b_recv[j - 1, rr], taken[rr][bits[j - 1][1]])
            along_z(j - 1)
        if j == CHUNKS - 3:
            for k in z_first:
                after_z(k)
                e[k].start()
    for j in z_first:
        e[j].wait_recv()
        for rr in range(ROUNDS):
            f_send[j, rr] = pick(c_recv[j, rr], e_recv[j, rr], taken[rr][bits[j][0]])
        f[j].start()
    for j in range(Z_FIRST, PARTS):
        after_z(j)
        d[j].start()
    for j in z_first:
        f[j].wait_recv()
        for rr in range(ROUNDS):
            g_send[j, rr] = pick(f_send[j, rr], f_recv[j, rr], taken[rr][bits[j][1]])
        d[j].start()

    def arrive(j, rr):
        return pick(landed[j][rr], d_recv[j, rr], taken[rr][0])

    for j in (*range(Z_FIRST, PARTS), *z_first):
        d[j].wait_recv()
        for rr in range(ROUNDS):
            other[rr, pl.ds(j * part, part)] = arrive(j, rr)
    after_z(PARTS)
    d[PARTS].start()
    for rr in range(ROUNDS):
        loss, slope = loss_and_slope(logits(img[...], other[rr], scale))
        losses[...] += loss
        igrad[...] += jnp.dot(slope.astype(jnp.bfloat16), other[rr], preferred_element_type=jnp.float32)
    igrad_out[...] = (igrad[...] * scale).astype(jnp.bfloat16)
    loss_out[...] = jnp.sum(losses[...].T, axis=0, keepdims=True) / ((ROUNDS + 1) * rows)
    for j in range(PARTS, CHUNKS):
        if j + 1 < CHUNKS:
            after_z(j + 1)
            d[j + 1].start()
        d[j].wait_recv()
        for rr in range(ROUNDS):
            arrived = arrive(j, rr)
            _, slope = loss_and_slope(logits(arrived, txt[...], scale))
            tgrad[...] += over_rows(slope.astype(jnp.bfloat16), arrived)
    tgrad_out[...] = (tgrad[...] * scale).astype(jnp.bfloat16)
    for j in range(CHUNKS):
        for sent in (*((e[j], f[j]) if j < Z_FIRST else (a[j], b[j])), *c[j], d[j]):
            sent.wait_send()


def whole_step(variant, scale, plan, images, texts):
    rows, width = images.shape
    part = rows // PARTS
    vmem = pl.BlockSpec(memory_space=pltpu.VMEM)
    both = pltpu.VMEM((CHUNKS, ROUNDS, part, width), jnp.bfloat16)
    early = pltpu.VMEM((Z_FIRST, ROUNDS, part, width), jnp.bfloat16)
    total = pltpu.VMEM((rows, width), jnp.float32)
    far_bits = (FAR, NEAR) if variant else (FAR,)
    return pl.pallas_call(
        functools.partial(kernel, far_bits, scale),
        out_shape=(
            jax.ShapeDtypeStruct((1, rows), jnp.float32),
            jax.ShapeDtypeStruct((rows, width), jnp.bfloat16),
            jax.ShapeDtypeStruct((rows, width), jnp.bfloat16),
        ),
        in_specs=[pl.BlockSpec(memory_space=pltpu.SMEM), vmem, vmem],
        out_specs=(vmem, vmem, vmem),
        scratch_shapes=[
            pltpu.VMEM((CHUNKS, part, width), jnp.bfloat16), both, both, both, both, both, early, early, early, early,
            pltpu.VMEM((ROUNDS, rows, width), jnp.bfloat16), pltpu.VMEM((rows, rows), jnp.float32), total, total,
            pltpu.SemaphoreType.DMA((2, CHUNKS)), pltpu.SemaphoreType.DMA((2, CHUNKS)),
            pltpu.SemaphoreType.DMA((2, CHUNKS, ROUNDS)), pltpu.SemaphoreType.DMA((2, CHUNKS)),
            pltpu.SemaphoreType.DMA((2, Z_FIRST)), pltpu.SemaphoreType.DMA((2, Z_FIRST)),
        ],
        compiler_params=pltpu.CompilerParams(
            collective_id=variant, has_side_effects=True, vmem_limit_bytes=48 * 2**20
        ),
        cost_estimate=pl.CostEstimate(flops=22 * rows * rows * width, bytes_accessed=8 * rows * width, transcendentals=0),
    )(plan, images, texts)


def hand_over(*arrays):
    def copies(*refs):
        n = len(arrays)
        moves = [pltpu.make_async_copy(refs[k], refs[n + k], refs[2 * n].at[k]) for k in range(n)]
        for move in moves:
            move.start()
        for move in moves:
            move.wait()

    anywhere = pl.BlockSpec(memory_space=pl.ANY)
    return pl.pallas_call(
        copies,
        out_shape=[jax.ShapeDtypeStruct(array.shape, array.dtype) for array in arrays],
        in_specs=[anywhere] * len(arrays),
        out_specs=[anywhere] * len(arrays),
        scratch_shapes=[pltpu.SemaphoreType.DMA((len(arrays),))],
    )(*arrays)


def kernel_shards(images, texts, plan):
    rows, width = images.shape
    scale = TEMPER / width**0.5
    crosses = jnp.bitwise_and(plan[0, 0], NEAR) != 0
    loss, igrad, tgrad = lax.cond(
        crosses, functools.partial(whole_step, 1, scale), functools.partial(whole_step, 0, scale), plan, images, texts
    )
    loss, igrad, tgrad = hand_over(loss, igrad, tgrad)
    return loss.reshape(rows), igrad, tgrad


def tile_coeffs(img, txt, labels, scale):
    z = jnp.dot(img, txt.T, preferred_element_type=jnp.float32) * scale + OFFSET
    loss = jnp.sum(jnp.logaddexp(jnp.float32(0.0), -labels * z), axis=1)
    g = (-labels * jax.nn.sigmoid(-labels * z)).astype(jnp.bfloat16)
    return (loss, g)


def coeffs(img, txt, labels, scale):
    z = jnp.dot(img, txt.T, preferred_element_type=jnp.float32) * scale + OFFSET
    return (-labels * jax.nn.sigmoid(-labels * z)).astype(jnp.bfloat16)


def image_side(g, txt, scale):
    return jnp.dot(g, txt, preferred_element_type=jnp.float32) * scale


def text_side(g, img, scale):
    return (
        lax.dot_general(g, img, (((0,), (0,)), ((), ())), preferred_element_type=jnp.float32)
        * scale
    )


def send_pairs(masks, *blocks):
    devices = range(lax.axis_size("dp"))
    return tuple(
        lax.ppermute(block, "dp", [(source, source ^ mask) for source in devices])
        if mask
        else block
        for block, mask in zip(blocks, masks)
    )


def exchange(images, texts, flips):
    nbits = lax.axis_size("dp").bit_length() - 1
    free = [nbits - 1 - rr for rr in range(ROUNDS)]
    digit_bits = HOP_BITS
    held = (images, texts) * ROUNDS
    low = 0
    while low < max(free):
        widths = [max(0, min(digit_bits, bits - low)) for bits in free]
        last = low + digit_bits >= max(free)
        index, count = jnp.int32(0), 1
        for rr, width in enumerate(widths):
            digit = jnp.bitwise_and(jnp.right_shift(flips[rr], low), 2**width - 1)
            index, count = index + digit * count, count * 2**width
        branches = []
        for branch in range(count):
            masks = []
            for bits, width in zip(free, widths):
                mask = (branch % 2**width) << low
                branch //= 2**width
                masks += [mask + (2**bits if last else 0)] * 2
            branches.append(lambda *blocks, masks=tuple(masks): send_pairs(masks, *blocks))
        held = lax.switch(index, branches, *held)
        low += digit_bits
    return [(held[2 * rr], held[2 * rr + 1]) for rr in range(ROUNDS)]


def hop_shards(images, texts, plan):
    rows_here, width = images.shape
    scale = TEMPER / width**0.5
    position = lax.axis_index("dp")
    flips = [jnp.bitwise_xor(plan[rr, position], position) for rr in range(ROUNDS)]
    eye = jnp.eye(rows_here, dtype=jnp.float32)
    diag_labels = 2.0 * eye - 1.0
    neg_labels = jnp.zeros((rows_here, rows_here), jnp.float32) - 1.0
    theirs = exchange(images, texts, flips)
    loss, g_diag = tile_coeffs(images, texts, diag_labels, scale)
    igrad = image_side(g_diag, texts, scale)
    tgrad = text_side(g_diag, images, scale)
    for other_img, other_txt in theirs:
        l2, g_mine = tile_coeffs(images, other_txt, neg_labels, scale)
        loss = loss + l2
        igrad = igrad + image_side(g_mine, other_txt, scale)
        g_theirs = coeffs(other_img, texts, neg_labels, scale)
        partial = text_side(g_theirs, other_img, scale).astype(jnp.bfloat16)
        tgrad = tgrad + partial.astype(jnp.float32)
    row_loss = loss / ((ROUNDS + 1) * rows_here)
    return (row_loss, igrad.astype(jnp.bfloat16), tgrad.astype(jnp.bfloat16))


def solution(mesh):
    placed = (P("dp", None), P("dp", None), P())
    return jax.shard_map(
        kernel_shards if mesh.shape["dp"] == KERNEL_DEVICES else hop_shards,
        mesh=mesh,
        in_specs=placed,
        out_specs=(P("dp"), P("dp", None), P("dp", None)),
        check_vma=False,
    )
```

```python
import functools

import jax
import jax.numpy as jnp
from jax import lax
from jax.experimental import pallas as pl
from jax.experimental.pallas import tpu as pltpu
from jax.sharding import PartitionSpec as P

MESH = pl.DeviceIdType.MESH
ROUNDS = 2
TEMPER = 2.0
OFFSET = -1.0
KERNEL_DEVICES = 32
CORE, FIRST, SECOND, NEAR, FAR = 1, 2, 4, 8, 16
PARTS = 4
CHUNKS = 2 * PARTS
Z_FIRST = 2
HOP_BITS = 2


def flip(index, bit):
    return index + bit - 2 * bit * ((index // bit) % 2)


def pick(own, other, taken):
    mixed = own.astype(jnp.float32) * (1.0 - taken) + other.astype(jnp.float32) * taken
    return mixed.astype(jnp.bfloat16)


def loss_and_slope(t):
    e = jnp.exp(-jnp.abs(t))
    r = 1.0 / (1.0 + e)
    return jnp.maximum(t, 0.0) + jnp.log1p(e), jnp.where(t >= 0.0, r, e * r)


def logits(img, txt, scale):
    dims = (((1,), (1,)), ((), ()))
    return lax.dot_general(img, txt, dims, preferred_element_type=jnp.float32) * scale + OFFSET


def over_rows(g, img):
    return lax.dot_general(g, img, (((0,), (0,)), ((), ())), preferred_element_type=jnp.float32)


def kernel(
    far_bits, scale, plan, img, txt, loss_out, igrad_out, tgrad_out,
    a_recv, b_send, b_recv, c_send, c_recv, d_recv, e_recv, f_send, f_recv, g_send, other, losses, igrad, tgrad,
    a_sems, b_sems, c_sems, d_sems, e_sems, f_sems,
):
    me = lax.axis_index("dp")
    core, first, second, near = (flip(me, bit) for bit in (CORE, FIRST, SECOND, NEAR))
    far = me
    for bit in far_bits:
        far = flip(far, bit)
    rows = img.shape[0]
    part = rows // PARTS
    taken = [
        [jnp.bitwise_and(lax.shift_right_logical(plan[rr, 0], bit), 1).astype(jnp.float32) for bit in range(3)]
        for rr in range(ROUNDS)
    ]

    barrier = pltpu.get_barrier_semaphore()
    for device in (core, first, second, near, far):
        pl.semaphore_signal(barrier, inc=1, device_id=(device,), device_id_type=MESH)
    pl.semaphore_wait(barrier, 5)

    def copy(src, dst, sems, place, device):
        return pltpu.make_async_remote_copy(
            src_ref=src, dst_ref=dst, send_sem=sems.at[(0, *place)], recv_sem=sems.at[(1, *place)],
            device_id=(device,), device_id_type=MESH,
        )

    def own(j):
        return (txt if j < PARTS else img).at[pl.ds((j % PARTS) * part, part)]

    plane_first, z_first = range(Z_FIRST, CHUNKS), range(Z_FIRST)
    order = [(first, second) if j % 2 == 0 else (second, first) for j in range(CHUNKS)]
    bits = [(1, 2) if j % 2 == 0 else (2, 1) for j in range(CHUNKS)]
    a = {j: copy(own(j), a_recv.at[j], a_sems, (j,), order[j][0]) for j in plane_first}
    b = {j: copy(b_send.at[j], b_recv.at[j], b_sems, (j,), order[j][1]) for j in plane_first}
    c = [
        [
            copy(own(j) if j < Z_FIRST else c_send.at[j, rr], c_recv.at[j, rr], c_sems, (j, rr), (far, near)[rr])
            for rr in range(ROUNDS)
        ]
        for j in range(CHUNKS)
    ]
    e = {j: copy(c_recv.at[j], e_recv.at[j], e_sems, (j,), order[j][0]) for j in z_first}
    f = {j: copy(f_send.at[j], f_recv.at[j], f_sems, (j,), order[j][1]) for j in z_first}
    landed = [g_send.at[j] if j < Z_FIRST else c_recv.at[j] for j in range(CHUNKS)]
    d = [copy(landed[j], d_recv.at[j], d_sems, (j,), core) for j in range(CHUNKS)]

    def diagonal():
        z = logits(img[...], txt[...], scale)
        shape = (rows, rows)
        same = lax.broadcasted_iota(jnp.int32, shape, 0) == lax.broadcasted_iota(jnp.int32, shape, 1)
        loss, slope = loss_and_slope(jnp.where(same, -z, z))
        losses[...] = loss
        g = jnp.where(same, -slope, slope).astype(jnp.bfloat16)
        igrad[...] = jnp.dot(g, txt[...], preferred_element_type=jnp.float32)
        tgrad[...] = over_rows(g, img[...])

    def along_z(j):
        for rr in range(ROUNDS):
            c[j][rr].start()

    def after_z(j):
        for rr in range(ROUNDS):
            c[j][rr].wait_recv()

    for j in z_first:
        along_z(j)
    for j in plane_first[:2]:
        a[j].start()
    diagonal()
    for j in range(Z_FIRST, CHUNKS + 1):
        if j < CHUNKS:
            a[j].wait_recv()
            for rr in range(ROUNDS):
                b_send[j, rr] = pick(own(j)[...], a_recv[j], taken[rr][bits[j][0]])
            b[j].start()
            if j + 2 < CHUNKS:
                a[j + 2].start()
        if j > Z_FIRST:
            b[j - 1].wait_recv()
            for rr in range(ROUNDS):
                c_send[j - 1, rr] = pick(b_send[j - 1, rr], b_recv[j - 1, rr], taken[rr][bits[j - 1][1]])
            along_z(j - 1)
        if j == CHUNKS - 3:
            for k in z_first:
                after_z(k)
                e[k].start()
    for j in z_first:
        e[j].wait_recv()
        for rr in range(ROUNDS):
            f_send[j, rr] = pick(c_recv[j, rr], e_recv[j, rr], taken[rr][bits[j][0]])
        f[j].start()
    for j in range(Z_FIRST, PARTS):
        after_z(j)
        d[j].start()
    for j in z_first:
        f[j].wait_recv()
        for rr in range(ROUNDS):
            g_send[j, rr] = pick(f_send[j, rr], f_recv[j, rr], taken[rr][bits[j][1]])
        d[j].start()

    def arrive(j, rr):
        return pick(landed[j][rr], d_recv[j, rr], taken[rr][0])

    for j in (*range(Z_FIRST, PARTS), *z_first):
        d[j].wait_recv()
        for rr in range(ROUNDS):
            other[rr, pl.ds(j * part, part)] = arrive(j, rr)
    after_z(PARTS)
    d[PARTS].start()
    for rr in range(ROUNDS):
        loss, slope = loss_and_slope(logits(img[...], other[rr], scale))
        losses[...] += loss
        igrad[...] += jnp.dot(slope.astype(jnp.bfloat16), other[rr], preferred_element_type=jnp.float32)
    igrad_out[...] = (igrad[...] * scale).astype(jnp.bfloat16)
    loss_out[...] = jnp.sum(losses[...].T, axis=0, keepdims=True) / ((ROUNDS + 1) * rows)
    for j in range(PARTS, CHUNKS):
        if j + 1 < CHUNKS:
            after_z(j + 1)
            d[j + 1].start()
        d[j].wait_recv()
        arrived = jnp.concatenate([arrive(j, rr) for rr in range(ROUNDS)], axis=0)
        _, slope = loss_and_slope(logits(arrived, txt[...], scale))
        tgrad[...] += over_rows(slope.astype(jnp.bfloat16), arrived)
    tgrad_out[...] = (tgrad[...] * scale).astype(jnp.bfloat16)
    for j in range(CHUNKS):
        for sent in (*((e[j], f[j]) if j < Z_FIRST else (a[j], b[j])), *c[j], d[j]):
            sent.wait_send()


def whole_step(variant, scale, plan, images, texts):
    rows, width = images.shape
    part = rows // PARTS
    vmem = pl.BlockSpec(memory_space=pltpu.VMEM)
    both = pltpu.VMEM((CHUNKS, ROUNDS, part, width), jnp.bfloat16)
    early = pltpu.VMEM((Z_FIRST, ROUNDS, part, width), jnp.bfloat16)
    total = pltpu.VMEM((rows, width), jnp.float32)
    far_bits = (FAR, NEAR) if variant else (FAR,)
    return pl.pallas_call(
        functools.partial(kernel, far_bits, scale),
        out_shape=(
            jax.ShapeDtypeStruct((1, rows), jnp.float32),
            jax.ShapeDtypeStruct((rows, width), jnp.bfloat16),
            jax.ShapeDtypeStruct((rows, width), jnp.bfloat16),
        ),
        in_specs=[pl.BlockSpec(memory_space=pltpu.SMEM), vmem, vmem],
        out_specs=(vmem, vmem, vmem),
        scratch_shapes=[
            pltpu.VMEM((CHUNKS, part, width), jnp.bfloat16), both, both, both, both, both, early, early, early, early,
            pltpu.VMEM((ROUNDS, rows, width), jnp.bfloat16), pltpu.VMEM((rows, rows), jnp.float32), total, total,
            pltpu.SemaphoreType.DMA((2, CHUNKS)), pltpu.SemaphoreType.DMA((2, CHUNKS)),
            pltpu.SemaphoreType.DMA((2, CHUNKS, ROUNDS)), pltpu.SemaphoreType.DMA((2, CHUNKS)),
            pltpu.SemaphoreType.DMA((2, Z_FIRST)), pltpu.SemaphoreType.DMA((2, Z_FIRST)),
        ],
        compiler_params=pltpu.CompilerParams(
            collective_id=variant, has_side_effects=True, vmem_limit_bytes=48 * 2**20
        ),
        cost_estimate=pl.CostEstimate(flops=22 * rows * rows * width, bytes_accessed=8 * rows * width, transcendentals=0),
    )(plan, images, texts)


def hand_over(*arrays):
    def copies(*refs):
        n = len(arrays)
        moves = [pltpu.make_async_copy(refs[k], refs[n + k], refs[2 * n].at[k]) for k in range(n)]
        for move in moves:
            move.start()
        for move in moves:
            move.wait()

    anywhere = pl.BlockSpec(memory_space=pl.ANY)
    return pl.pallas_call(
        copies,
        out_shape=[jax.ShapeDtypeStruct(array.shape, array.dtype) for array in arrays],
        in_specs=[anywhere] * len(arrays),
        out_specs=[anywhere] * len(arrays),
        scratch_shapes=[pltpu.SemaphoreType.DMA((len(arrays),))],
    )(*arrays)


def kernel_shards(images, texts, plan):
    rows, width = images.shape
    scale = TEMPER / width**0.5
    crosses = jnp.bitwise_and(plan[0, 0], NEAR) != 0
    loss, igrad, tgrad = lax.cond(
        crosses, functools.partial(whole_step, 1, scale), functools.partial(whole_step, 0, scale), plan, images, texts
    )
    loss, igrad, tgrad = hand_over(loss, igrad, tgrad)
    return loss.reshape(rows), igrad, tgrad


def tile_coeffs(img, txt, labels, scale):
    z = jnp.dot(img, txt.T, preferred_element_type=jnp.float32) * scale + OFFSET
    loss = jnp.sum(jnp.logaddexp(jnp.float32(0.0), -labels * z), axis=1)
    g = (-labels * jax.nn.sigmoid(-labels * z)).astype(jnp.bfloat16)
    return (loss, g)


def coeffs(img, txt, labels, scale):
    z = jnp.dot(img, txt.T, preferred_element_type=jnp.float32) * scale + OFFSET
    return (-labels * jax.nn.sigmoid(-labels * z)).astype(jnp.bfloat16)


def image_side(g, txt, scale):
    return jnp.dot(g, txt, preferred_element_type=jnp.float32) * scale


def text_side(g, img, scale):
    return (
        lax.dot_general(g, img, (((0,), (0,)), ((), ())), preferred_element_type=jnp.float32)
        * scale
    )


def send_pairs(masks, *blocks):
    devices = range(lax.axis_size("dp"))
    return tuple(
        lax.ppermute(block, "dp", [(source, source ^ mask) for source in devices])
        if mask
        else block
        for block, mask in zip(blocks, masks)
    )


def exchange(images, texts, flips):
    nbits = lax.axis_size("dp").bit_length() - 1
    free = [nbits - 1 - rr for rr in range(ROUNDS)]
    digit_bits = HOP_BITS
    held = (images, texts) * ROUNDS
    low = 0
    while low < max(free):
        widths = [max(0, min(digit_bits, bits - low)) for bits in free]
        last = low + digit_bits >= max(free)
        index, count = jnp.int32(0), 1
        for rr, width in enumerate(widths):
            digit = jnp.bitwise_and(jnp.right_shift(flips[rr], low), 2**width - 1)
            index, count = index + digit * count, count * 2**width
        branches = []
        for branch in range(count):
            masks = []
            for bits, width in zip(free, widths):
                mask = (branch % 2**width) << low
                branch //= 2**width
                masks += [mask + (2**bits if last else 0)] * 2
            branches.append(lambda *blocks, masks=tuple(masks): send_pairs(masks, *blocks))
        held = lax.switch(index, branches, *held)
        low += digit_bits
    return [(held[2 * rr], held[2 * rr + 1]) for rr in range(ROUNDS)]


def hop_shards(images, texts, plan):
    rows_here, width = images.shape
    scale = TEMPER / width**0.5
    position = lax.axis_index("dp")
    flips = [jnp.bitwise_xor(plan[rr, position], position) for rr in range(ROUNDS)]
    eye = jnp.eye(rows_here, dtype=jnp.float32)
    diag_labels = 2.0 * eye - 1.0
    neg_labels = jnp.zeros((rows_here, rows_here), jnp.float32) - 1.0
    theirs = exchange(images, texts, flips)
    loss, g_diag = tile_coeffs(images, texts, diag_labels, scale)
    igrad = image_side(g_diag, texts, scale)
    tgrad = text_side(g_diag, images, scale)
    for other_img, other_txt in theirs:
        l2, g_mine = tile_coeffs(images, other_txt, neg_labels, scale)
        loss = loss + l2
        igrad = igrad + image_side(g_mine, other_txt, scale)
        g_theirs = coeffs(other_img, texts, neg_labels, scale)
        partial = text_side(g_theirs, other_img, scale).astype(jnp.bfloat16)
        tgrad = tgrad + partial.astype(jnp.float32)
    row_loss = loss / ((ROUNDS + 1) * rows_here)
    return (row_loss, igrad.astype(jnp.bfloat16), tgrad.astype(jnp.bfloat16))


def solution(mesh):
    placed = (P("dp", None), P("dp", None), P())
    return jax.shard_map(
        kernel_shards if mesh.shape["dp"] == KERNEL_DEVICES else hop_shards,
        mesh=mesh,
        in_specs=placed,
        out_specs=(P("dp"), P("dp", None), P("dp", None)),
        check_vma=False,
    )
```
